128 devices in a mesh: node: 8 (over y, core), local: 16 (over x, z).
Axes of the slice: x: 4, y: 4, z: 4, core: 2. Of those that a mesh axis runs over, the one named last changes fastest.
Arguments:
- tokens: bfloat16 [8192, 3584], P(('node', 'local')), may hold values from -6 to 6
- expert_ids: int32 [8192, 8], P(('node', 'local')), may hold values from 0 to 127, as said below
- gate_values: bfloat16 [8192, 8], P(('node', 'local')), may hold values from 0.049804688 to 0.44921875
- expert_gate: bfloat16 [128, 3584, 1024], P(('node', 'local')), may hold values from -0.09375 to 0.09375
- expert_up: bfloat16 [128, 3584, 1024], P(('node', 'local')), may hold values from -0.09375 to 0.09375
- expert_down: bfloat16 [128, 1024, 3584], P(('node', 'local')), may hold values from -0.1875 to 0.1875
Outputs:
- mixed: bfloat16 [8192, 3584], P(('node', 'local'))
The draws below stay inside these ranges and needn't reach their ends.
Inputs may be any that keep to these rules, and one draw needn't show every extreme that they name: `expert_ids`: each row names 8 different experts, the same number on each of exactly 4 nodes. Among the rows of one device, each node is named by exactly 32 rows, no expert is named more than 8 times, and on every node some expert is named exactly 8 times.
All inputs are finite; a program needn't handle non-finite values.
Results may differ from the reference program's by a relative error of at most 0.012.
Values may be sent and summed in bfloat16 or wider, within the bound.
No kernel may reach another device: no remote copies, remote signals or barrier semaphores. Data moves between devices by JAX's collectives and lax.ppermute only.
A program may use at most 128 MiB of HBM per device.

```python
import jax
import jax.numpy as jnp
from jax import lax

D = 3584
FF = 1024
TOPK = 8
NODES_HIT = 4
TOK_DEV = 64
EXPERTS = 128
CAP = 8
TOKENS = 8192
N_NODE = 8
N_LOCAL = 16


def route_block(block_key):
    band = TOK_DEV // N_NODE
    pair = TOPK // NODES_HIT
    key_nodes, key_place, key_local = jax.random.split(block_key, 3)
    node_order = jax.random.permutation(key_nodes, N_NODE).astype(jnp.int32)
    token_place = jax.random.permutation(key_place, TOK_DEV).astype(jnp.int32)
    local_keys = jax.random.split(key_local, N_NODE)
    local_orders = jax.vmap(lambda k: jax.random.permutation(k, N_LOCAL).astype(jnp.int32))(local_keys)
    start = token_place % N_NODE
    band_index = token_place // N_NODE
    window = jnp.arange(NODES_HIT, dtype=jnp.int32)
    slot_node = (start[:, None] + window[None, :]) % N_NODE
    rank = window[None, :] * band + band_index[:, None]
    busy = rank < CAP
    others = N_LOCAL - 1
    stream = CAP + 2 * (rank - CAP)
    first = jnp.where(busy, 0, 1 + stream % others)
    second = jnp.where(busy, 1 + rank % others, 1 + (stream + 1) % others)
    orders = local_orders[slot_node]
    local_a = jnp.take_along_axis(orders, first[:, :, None], axis=2)[:, :, 0]
    local_b = jnp.take_along_axis(orders, second[:, :, None], axis=2)[:, :, 0]
    node = node_order[slot_node]
    chosen = jnp.stack([node * N_LOCAL + local_a, node * N_LOCAL + local_b], axis=2)
    return chosen.reshape(TOK_DEV, NODES_HIT * pair).astype(jnp.int32)


def draw_expert_ids(key, part):
    key = jax.random.fold_in(key, 11)
    block_keys = jax.random.split(key, TOKENS // TOK_DEV)
    blocks = jax.vmap(route_block)(block_keys)
    return blocks.reshape(TOKENS, TOPK).astype(jnp.int32)


def steps_of(stream_key, shape, shards, smallest, top_value):
    loudness = 1.0
    for dim, shards_of in shards:
        steps = jax.random.uniform(jax.random.fold_in(jax.random.fold_in(stream_key, 6), dim), (shards_of,), jnp.float32, smallest / len(shards), top_value / len(shards))
        loudness = loudness * jnp.repeat(jnp.exp(steps), shape[dim] // shards_of).reshape((-1,) + (1,) * (len(shape) - 1 - dim))
    return loudness


def gaussian(stream_key, dims, scale, most, pieces=(), kind=jnp.bfloat16):
    factor_of = steps_of(stream_key, dims, pieces, -0.22, 0.18) if pieces else 1.0
    drawn = jax.random.normal(stream_key, dims, jnp.float32) * scale * factor_of
    return jnp.minimum(jnp.maximum(drawn, -most), most).astype(kind)


def setup_inputs(seed: int = 0) -> dict:
    arg_keys = jax.random.split(jax.random.key(seed), 7)
    return {
        "tokens": gaussian(arg_keys[0], (TOKENS, D), 1.0, 6.0, ((0, 128),)),
        "expert_ids": draw_expert_ids(jax.random.fold_in(arg_keys[6], 71), 0),
        "gate_values": jnp.clip(0.049804688 + 0.39941406 * jax.random.uniform(arg_keys[2], (TOKENS, TOPK), jnp.float32) ** steps_of(arg_keys[2], (TOKENS, TOPK), ((0, 128),), -0.2, 0.2), 0.049804688, 0.44921875).astype(jnp.bfloat16),
        "expert_gate": gaussian(arg_keys[3], (EXPERTS, D, FF), D ** -0.5, 0.09375, ((0, 128),)),
        "expert_up": gaussian(arg_keys[4], (EXPERTS, D, FF), D ** -0.5, 0.09375, ((0, 128),)),
        "expert_down": gaussian(arg_keys[5], (EXPERTS, FF, D), FF ** -0.5, 0.1875, ((0, 128),)),
    }


def expert_apply(rows, w_gate, w_up, w_down):
    gate_rows = jnp.dot(rows, w_gate, preferred_element_type=jnp.float32)
    up_rows = jnp.dot(rows, w_up, preferred_element_type=jnp.float32)
    hidden = (jax.nn.silu(gate_rows) * up_rows).astype(jnp.bfloat16)
    return jnp.dot(hidden, w_down, preferred_element_type=jnp.float32).astype(jnp.bfloat16)


def reference(tokens, expert_ids, gate_values, expert_gate, expert_up, expert_down):
    room = EXPERTS * CAP
    flat_ids = expert_ids.reshape(-1).astype(jnp.int32)
    order = jnp.argsort(flat_ids, stable=True).astype(jnp.int32)
    counts = jnp.bincount(flat_ids, length=EXPERTS).astype(jnp.int32)
    starts = (jnp.cumsum(counts) - counts).astype(jnp.int32)
    padded_order = jnp.concatenate([order, jnp.zeros((room,), jnp.int32)])
    gates_flat = gate_values.reshape(-1).astype(jnp.float32)
    positions = jnp.arange(room, dtype=jnp.int32)

    def node_sum(node):
        def step(total, local):
            expert = (node * N_LOCAL + local).astype(jnp.int32)
            picked = lax.dynamic_slice(padded_order, (starts[expert].astype(jnp.int32),), (room,))
            live = positions < counts[expert]
            token_index = (picked // TOPK).astype(jnp.int32)
            outputs = expert_apply(tokens[token_index], expert_gate[expert], expert_up[expert], expert_down[expert])
            weight = jnp.where(live, gates_flat[picked], jnp.float32(0.0))
            total = total.at[token_index].add(weight[:, None] * outputs.astype(jnp.float32))
            return total, None

        start = jnp.zeros((TOKENS, D), jnp.float32)
        total, _ = lax.scan(step, start, jnp.arange(N_LOCAL, dtype=jnp.int32))
        rounded = lax.optimization_barrier(total.astype(jnp.bfloat16))
        return rounded.astype(jnp.float32)

    def add_node(node, mixed_sum):
        return mixed_sum + node_sum(jnp.int32(node))

    mixed_sum = lax.fori_loop(0, N_NODE, add_node, jnp.zeros((TOKENS, D), jnp.float32))
    return mixed_sum.astype(jnp.bfloat16)
```

```python
import jax
import jax.numpy as jnp
from jax import lax
from jax.sharding import PartitionSpec as P

BOTH = ("node", "local")
RING = 4
LANES = 128

OFFSETS = ((0, 1, 3, 2), (0, 3, 1, 2))

ORDERS = (("z", "x", "y"), ("y", "z", "x"), ("x", "y", "z"))
AXES = ("y", "x", "z")


def index_of(y, c, x, z):
    return ((y * 2 + c) * RING + x) * RING + z


def pairs(axis, k):
    out = []
    for y in range(RING):
        for c in range(2):
            for x in range(RING):
                for z in range(RING):
                    at = {"y": y, "x": x, "z": z}
                    at[axis] ^= OFFSETS[c][k]
                    out.append((index_of(y, c, x, z), index_of(at["y"], c, at["x"], at["z"])))
    return out


def to_partner(value, axis, k):
    return lax.ppermute(value, BOTH, pairs(axis, k))


def to_other_core(value):
    swap = [(i, i ^ 16) for i in range(128)]
    return lax.ppermute(value, BOTH, swap)


def gather_ring(block, axis):
    pair = jnp.concatenate([block, to_partner(block, axis, 1)], axis=0)
    return jnp.concatenate([pair, to_partner(pair, axis, 2)], axis=0)


def add(a, b):
    return (a.astype(jnp.float32) + b.astype(jnp.float32)).astype(jnp.bfloat16)


def reduce_ring(blocks, axis):
    half = blocks.shape[0] // 2
    pair = add(blocks[:half], to_partner(blocks[half:], axis, 2))
    half = half // 2
    return add(pair[:half], to_partner(pair[half:], axis, 1))


def column_chunks(width):
    tiles = width // LANES
    cuts = [(tiles * i + 2) // 3 * LANES for i in range(3)] + [width]
    cuts[0] = 0
    return [(cuts[i], cuts[i + 1] - cuts[i]) for i in range(3)]


def shards(tokens, expert_ids, gate_values, expert_gate, expert_up, expert_down):
    node = lax.axis_index("node")
    local = lax.axis_index("local")
    at = {"y": node // 2, "x": local // RING, "z": local % RING}
    core = node % 2
    experts = lax.axis_size("node") * lax.axis_size("local")
    tok, width = tokens.shape
    top = expert_ids.shape[1]
    cap = 2 * tok * top // experts

    hits = (expert_ids[:, :, None] == jnp.arange(experts, dtype=jnp.int32)).astype(jnp.int32)
    named = jnp.sum(hits, axis=1)
    earlier = jnp.cumsum(named, axis=0) - named
    slot = jnp.sum(hits * earlier[:, None, :], axis=2)
    place = (expert_ids * cap + slot).astype(jnp.float32)
    about = jnp.concatenate([place, gate_values.astype(jnp.float32)], axis=1)
    about = lax.all_gather(about, BOTH)

    mine = jnp.where(core == 0, jnp.array(OFFSETS[0]), jnp.array(OFFSETS[1])).astype(jnp.int32)
    ring = jnp.arange(RING)

    def selection(order):
        first, second, last = order
        coord = {last: at[last], second: at[second] ^ mine[:, None], first: at[first] ^ mine[None, :]}
        source = index_of(coord["y"], core, coord["x"], coord["z"])
        source = jnp.broadcast_to(source, (RING, RING)).reshape(-1)
        known = jnp.take(about, source, axis=0)
        place = known[:, :, :top].astype(jnp.int32)
        weight = known[:, :, top:]
        held = jnp.arange(RING * RING, dtype=jnp.int32)
        have = (held[:, None, None] * (experts * cap) + place).reshape(-1, top)
        spot = dict(at)
        spot[last] = at[last] ^ mine
        expert = index_of(spot["y"], core, spot["x"], spot["z"])
        expert = jnp.stack([expert, expert ^ 16], axis=1)
        grid = held.reshape(RING, RING)
        if AXES.index(first) < AXES.index(second):
            grid = grid.T
        grid = grid.reshape(-1)
        want = (
            grid[None, None, :, None] * (experts * cap)
            + expert[:, :, None, None] * cap
            + jnp.arange(cap, dtype=jnp.int32)
        ).reshape(RING, -1)
        same = want[:, :, None, None] == have.T[None, None, :, :]
        chosen = jnp.any(same, axis=2).astype(jnp.bfloat16)
        weights = jnp.sum(
            jnp.where(same, weight.reshape(-1, top).T[None, None], jnp.float32(0.0)), axis=2
        ).astype(jnp.bfloat16)
        return chosen, weights

    chunks = column_chunks(width)
    picks = [selection(order) for order in ORDERS]

    def arrange(pieces, last):
        return jnp.stack(pieces, axis=AXES.index(last))

    def forward(number):
        start, size = chunks[number]
        first, second, last = ORDERS[number]
        chosen = picks[number][0]
        held = gather_ring(gather_ring(tokens[:, start : start + size], first), second)
        own, other = [], []
        for k in range(RING):
            rows = jnp.dot(chosen[k], held, preferred_element_type=jnp.float32).astype(jnp.bfloat16)
            if k:
                rows = to_partner(rows, last, k)
            half = rows.shape[0] // 2
            own.append(rows[:half])
            other.append(rows[half:])
        other = to_other_core(jnp.concatenate(other, axis=0))
        other = list(other.reshape(RING, -1, size))
        shape = (RING, RING, cap, size)
        both = [arrange([p.reshape(shape) for p in part], last).reshape(-1, size) for part in (own, other)]
        return jnp.concatenate(both, axis=0)

    rows = jnp.concatenate([forward(i) for i in range(3)], axis=1)
    gate_rows = jnp.dot(rows, expert_gate[0], preferred_element_type=jnp.float32)
    up_rows = jnp.dot(rows, expert_up[0], preferred_element_type=jnp.float32)
    hidden = (jax.nn.silu(gate_rows) * up_rows).astype(jnp.bfloat16)

    def backward(number):
        start, size = chunks[number]
        first, second, last = ORDERS[number]
        weights = picks[number][1]
        out = jnp.dot(
            hidden, expert_down[0][:, start : start + size], preferred_element_type=jnp.float32
        ).astype(jnp.bfloat16)
        out = out.reshape(2, RING, RING, RING, cap, size)
        out = jnp.moveaxis(out, 1 + AXES.index(last), 1)
        own = out[0].reshape(RING, -1, size)
        other = to_other_core(out[1].reshape(RING, -1, size))
        total = 0.0
        for k in range(RING):
            rows = jnp.concatenate([own[k], other[k]], axis=0)
            if k:
                rows = to_partner(rows, last, k)
            total = total + lax.dot_general(
                weights[k], rows, (((0,), (0,)), ((), ())), preferred_element_type=jnp.float32
            )
        return reduce_ring(reduce_ring(total.astype(jnp.bfloat16), second), first)

    return jnp.concatenate([backward(i) for i in range(3)], axis=1)


def solution(mesh):
    placed = (
        P(BOTH, None),
        P(BOTH, None),
        P(BOTH, None),
        P(BOTH, None, None),
        P(BOTH, None, None),
        P(BOTH, None, None),
    )
    return jax.shard_map(
        shards, mesh=mesh, in_specs=placed, out_specs=P(BOTH, None), check_vma=False
    )
```

```python
import jax
import jax.numpy as jnp
from jax import lax
from jax.sharding import PartitionSpec as P

BOTH = ("node", "local")
RING = 4
CORES = 2
LANES = 128

GATHER = (1, 3)
EXCHANGE = (3, 1)

NEAR = ((0, 0, 0), (1, 0, 0), (0, 1, 0), (0, 0, 1))
FAR = ((1, 1, 0), (0, 1, 1), (1, 0, 1), (1, 1, 1))
CORNERS = tuple((i >> 2 & 1, i >> 1 & 1, i & 1) for i in range(8))


def index_of(y, c, x, z):
    return ((y * CORES + c) * RING + x) * RING + z


def places():
    return [
        (y, c, x, z) for y in range(RING) for c in range(CORES) for x in range(RING) for z in range(RING)
    ]


def moved(place, corner, step):
    y, c, x, z = place
    return index_of(y ^ corner[0] * step, c, x ^ corner[1] * step, z ^ corner[2] * step)


def to_corner(value, corner):
    return lax.ppermute(value, BOTH, [(index_of(*p), moved(p, corner, GATHER[p[1]])) for p in places()])


def to_other_core(value):
    return lax.ppermute(
        value, BOTH, [(index_of(y, c, x, z), index_of(y, 1 - c, x, z)) for y, c, x, z in places()]
    )


def first_of(v, core):
    return (v if v < 2 else v ^ 3) if core == 0 else v & 2


def exchange(value):
    groups = [
        [moved((y, c, x, z), corner, EXCHANGE[c]) for corner in CORNERS]
        for y, c, x, z in places()
        if all(first_of(v, c) == v for v in (y, x, z))
    ]
    return lax.all_to_all(
        value, BOTH, split_axis=0, concat_axis=0, axis_index_groups=groups, tiled=True
    )


def gather_cube(block):
    y, x, z = [to_corner(block, corner) for corner in NEAR[1:]]
    far = [to_corner(x, NEAR[1]), to_corner(z, NEAR[2]), to_corner(y, NEAR[3]), to_corner(block, FAR[3])]
    return [block, y, x, z] + far


def add(a, *others):
    total = a.astype(jnp.float32)
    for b in others:
        total = total + b.astype(jnp.float32)
    return total.astype(jnp.bfloat16)


def reduce_cube(blocks):
    own, y, x, z, yx, xz, yz, yxz = blocks
    x = add(x, to_corner(yx, NEAR[1]))
    z = add(z, to_corner(xz, NEAR[2]))
    y = add(y, to_corner(yz, NEAR[3]))
    last = to_corner(yxz, FAR[3])
    return add(own, last, *[to_corner(b, corner) for b, corner in zip((y, x, z), NEAR[1:])])


def shards(tokens, expert_ids, gate_values, expert_gate, expert_up, expert_down):
    node = lax.axis_index("node")
    local = lax.axis_index("local")
    at = (node // CORES, local // RING, local % RING)
    core = node % CORES
    experts = lax.axis_size("node") * lax.axis_size("local")
    tok, width = tokens.shape
    top = expert_ids.shape[1]
    cap = 2 * tok * top // experts
    corners = len(CORNERS)
    held = corners * tok

    hits = (expert_ids[:, :, None] == jnp.arange(experts, dtype=jnp.int32)).astype(jnp.int32)
    named = jnp.sum(hits, axis=1)
    earlier = jnp.cumsum(named, axis=0) - named
    slot = jnp.sum(hits * earlier[:, None, :], axis=2)
    about = jnp.concatenate(
        [expert_ids.astype(jnp.bfloat16), slot.astype(jnp.bfloat16), gate_values], axis=1
    )
    about = jnp.pad(about, ((0, 0), (0, LANES - 3 * top)))

    blocks = gather_cube(jnp.concatenate([tokens, about], axis=1))
    rows = jnp.concatenate([b[:, :width] for b in blocks], axis=0)
    known = jnp.concatenate([b[:, width:] for b in blocks], axis=0)

    step = jnp.where(core == 0, EXCHANGE[0], EXCHANGE[1])
    base = [jnp.where(core == 0, jnp.where(v < 2, v, v ^ 3), v & 2) for v in at]
    bits = jnp.array(CORNERS, dtype=jnp.int32)
    spot = [base[i] ^ (bits[:, i] * step) for i in range(3)]
    wanted = index_of(spot[0], core, spot[1], spot[2])
    wanted = jnp.stack([wanted, wanted ^ (RING * RING)], axis=1)[:, :, None] * cap + jnp.arange(cap, dtype=jnp.int32)
    wanted = wanted.reshape(-1, 1).astype(jnp.float32)

    known = known.astype(jnp.float32).T[: 3 * top].reshape(3, top, held)
    place = known[0] * cap + known[1]
    chosen = jnp.zeros((wanted.shape[0], held), jnp.float32)
    weights = chosen
    for k in range(top):
        same = wanted == place[k][None, :]
        chosen = jnp.where(same, jnp.float32(1.0), chosen)
        weights = jnp.where(same, known[2, k][None, :], weights)

    source = jnp.repeat(jnp.arange(corners, dtype=jnp.int32), tok)
    mask = jnp.arange(corners, dtype=jnp.int32)[:, None, None] == source[None, None, :]

    def spread(small):
        small = small.reshape(corners * CORES, 1, cap, held)
        wide = jnp.where(mask[None], small, jnp.float32(0.0)).astype(jnp.bfloat16)
        return wide.reshape(corners * CORES * corners * cap, held)

    half = corners * cap
    send = jnp.dot(spread(chosen), rows, preferred_element_type=jnp.float32).astype(jnp.bfloat16)
    got = exchange(send.reshape(corners, CORES * half, width))
    theirs = to_other_core(got[:, half:].reshape(corners * half, width))
    mine = got[:, :half].reshape(corners * half, width)

    def inner(rows):
        gate_rows = jnp.dot(rows, expert_gate[0], preferred_element_type=jnp.float32)
        up_rows = jnp.dot(rows, expert_up[0], preferred_element_type=jnp.float32)
        return (jax.nn.silu(gate_rows) * up_rows).astype(jnp.bfloat16)

    def outer(hidden):
        out = jnp.dot(hidden, expert_down[0], preferred_element_type=jnp.float32).astype(jnp.bfloat16)
        return out.reshape(corners, half, width)

    hidden = inner(mine)
    theirs = to_other_core(outer(inner(theirs)))
    back = exchange(jnp.concatenate([outer(hidden), theirs], axis=1))
    total = lax.dot_general(
        spread(weights),
        back.reshape(corners * CORES * half, width),
        (((0,), (0,)), ((), ())),
        preferred_element_type=jnp.float32,
    ).astype(jnp.bfloat16)
    return reduce_cube([total[i * tok : (i + 1) * tok] for i in range(corners)])


def solution(mesh):
    placed = (
        P(("node", "local"), None),
        P(("node", "local"), None),
        P(("node", "local"), None),
        P(("node", "local"), None, None),
        P(("node", "local"), None, None),
        P(("node", "local"), None, None),
    )
    return jax.shard_map(
        shards, mesh=mesh, in_specs=placed, out_specs=P(("node", "local"), None), check_vma=False
    )
```

```python
import functools

import jax
import jax.numpy as jnp
from jax import lax
from jax.experimental import pallas as pl
from jax.experimental.pallas import tpu as pltpu
from jax.sharding import PartitionSpec as P

BOTH = ("node", "local")
RING = 4
CORES = 2
LANES = 128

GATHER = (1, 3)
EXCHANGE = (3, 1)

NEAR = ((0, 0, 0), (1, 0, 0), (0, 1, 0), (0, 0, 1))
FAR = ((1, 1, 0), (0, 1, 1), (1, 0, 1), (1, 1, 1))
CORNERS = tuple((i >> 2 & 1, i >> 1 & 1, i & 1) for i in range(8))


def index_of(y, c, x, z):
    return ((y * CORES + c) * RING + x) * RING + z


def places():
    return [
        (y, c, x, z) for y in range(RING) for c in range(CORES) for x in range(RING) for z in range(RING)
    ]


def moved(place, corner, step):
    y, c, x, z = place
    return index_of(y ^ corner[0] * step, c, x ^ corner[1] * step, z ^ corner[2] * step)


def to_corner(value, corner):
    return lax.ppermute(value, BOTH, [(index_of(*p), moved(p, corner, GATHER[p[1]])) for p in places()])


def to_other_core(value):
    return lax.ppermute(
        value, BOTH, [(index_of(y, c, x, z), index_of(y, 1 - c, x, z)) for y, c, x, z in places()]
    )


def first_of(v, core):
    return (v if v < 2 else v ^ 3) if core == 0 else v & 2


def exchange(value, flip):
    groups = [
        [moved((y, c, x, z), corner, EXCHANGE[c ^ flip]) for corner in CORNERS]
        for y, c, x, z in places()
        if all(first_of(v, c ^ flip) == v for v in (y, x, z))
    ]
    return lax.all_to_all(
        value, BOTH, split_axis=0, concat_axis=0, axis_index_groups=groups, tiled=True
    )


def gather_cube(block):
    y, x, z = [to_corner(block, corner) for corner in NEAR[1:]]
    far = [to_corner(x, NEAR[1]), to_corner(z, NEAR[2]), to_corner(y, NEAR[3]), to_corner(block, FAR[3])]
    return [block, y, x, z] + far


def add(a, *others):
    total = a.astype(jnp.float32)
    for b in others:
        total = total + b.astype(jnp.float32)
    return total.astype(jnp.bfloat16)


def reduce_cube(blocks):
    own, y, x, z, yx, xz, yz, yxz = blocks
    x = add(x, to_corner(yx, NEAR[1]))
    z = add(z, to_corner(xz, NEAR[2]))
    y = add(y, to_corner(yz, NEAR[3]))
    last = to_corner(yxz, FAR[3])
    return add(own, last, *[to_corner(b, corner) for b, corner in zip((y, x, z), NEAR[1:])])


def stack_kernel(count, *refs):
    size = refs[0].shape[0]
    rows_ref, about_ref = refs[2 * count :]
    for i in range(count):
        rows_ref[i * size : (i + 1) * size] = refs[i][...]

    @pl.when(pl.program_id(0) == 0)
    def _():
        for i in range(count):
            about_ref[i * size : (i + 1) * size] = refs[count + i][...]


def stack(blocks, width):
    count, size = len(blocks), blocks[0].shape[0]
    rest = blocks[0].shape[1] - width
    dtype = blocks[0].dtype
    wide = 896
    return pl.pallas_call(
        functools.partial(stack_kernel, count),
        grid=(width // wide,),
        in_specs=[pl.BlockSpec((size, wide), lambda i: (0, i))] * count
        + [pl.BlockSpec((size, rest), lambda i: (0, width // rest))] * count,
        out_specs=[
            pl.BlockSpec((count * size, wide), lambda i: (0, i)),
            pl.BlockSpec((count * size, rest), lambda i: (0, 0)),
        ],
        out_shape=[
            jax.ShapeDtypeStruct((count * size, width), dtype),
            jax.ShapeDtypeStruct((count * size, rest), dtype),
        ],
        compiler_params=pltpu.CompilerParams(vmem_limit_bytes=32 * 2**20),
        name="stack",
    )(*blocks, *blocks)


def follow_kernel(value_ref, after_ref, out_ref):
    del value_ref, after_ref, out_ref


def follow(value, after):
    return pl.pallas_call(
        follow_kernel,
        in_specs=[pl.BlockSpec(memory_space=pl.ANY)] * 2,
        out_specs=pl.BlockSpec(memory_space=pl.ANY),
        out_shape=jax.ShapeDtypeStruct(value.shape, value.dtype),
        input_output_aliases={0: 0},
        name="follow",
    )(value, after)


def expert_kernel(inner, tile, after_ref, rows_ref, gate_ref, up_ref, down_ref, out_ref, hidden):
    del after_ref
    step = pl.program_id(0)

    @pl.when(step < inner)
    def _():
        gate = jnp.dot(rows_ref[...], gate_ref[...], preferred_element_type=jnp.float32)
        up = jnp.dot(rows_ref[...], up_ref[...], preferred_element_type=jnp.float32)
        columns = pl.ds(pl.multiple_of(step * tile, tile), tile)
        hidden[:, columns] = (gate / (1.0 + jnp.exp(-gate)) * up).astype(hidden.dtype)

    @pl.when(step >= inner)
    def _():
        out = jnp.dot(hidden[...], down_ref[...], preferred_element_type=jnp.float32)
        out_ref[...] = out.astype(out_ref.dtype)


def expert(rows, gate, up, down, after):
    count, width = rows.shape
    hidden = gate.shape[1]
    tile = 256
    wide = 512
    inner, outer = hidden // tile, width // wide

    def of_inner(i):
        return 0, jnp.minimum(i, inner - 1)

    def of_outer(i):
        return 0, jnp.maximum(i - inner, 0)

    return pl.pallas_call(
        functools.partial(expert_kernel, inner, tile),
        grid=(inner + outer,),
        in_specs=[
            pl.BlockSpec(memory_space=pl.ANY),
            pl.BlockSpec((count, width), lambda i: (0, 0)),
            pl.BlockSpec((width, tile), of_inner),
            pl.BlockSpec((width, tile), of_inner),
            pl.BlockSpec((hidden, wide), of_outer),
        ],
        out_specs=pl.BlockSpec((count, wide), of_outer),
        out_shape=jax.ShapeDtypeStruct((count, width), rows.dtype),
        scratch_shapes=[pltpu.VMEM((count, hidden), rows.dtype)],
        compiler_params=pltpu.CompilerParams(vmem_limit_bytes=48 * 2**20),
        cost_estimate=pl.CostEstimate(
            flops=6 * count * width * hidden,
            bytes_accessed=2 * (3 * width * hidden + 2 * count * width),
            transcendentals=count * hidden,
        ),
        name="expert",
    )(after, rows, gate, up, down)


def shards(tokens, expert_ids, gate_values, expert_gate, expert_up, expert_down):
    node = lax.axis_index("node")
    local = lax.axis_index("local")
    at = (node // CORES, local // RING, local % RING)
    core = node % CORES
    experts = lax.axis_size("node") * lax.axis_size("local")
    tok, width = tokens.shape
    top = expert_ids.shape[1]
    cap = 2 * tok * top // experts
    corners = len(CORNERS)
    held = corners * tok

    about = jnp.concatenate([expert_ids.astype(jnp.bfloat16), gate_values], axis=1)
    about = jnp.pad(about, ((0, 0), (0, LANES - 2 * top)))
    own_held, own_known = stack(gather_cube(jnp.concatenate([tokens, about], axis=1)), width)
    other_held = to_other_core(own_held)
    other_known = to_other_core(own_known)

    bits = jnp.array(CORNERS, dtype=jnp.int32)
    source = jnp.repeat(jnp.arange(corners, dtype=jnp.int32), tok)
    mask = jnp.arange(corners, dtype=jnp.int32)[:, None, None] == source[None, None, :]
    order = jnp.arange(held, dtype=jnp.int32)
    earlier = (order[:, None] < order[None, :]) & (source[:, None] == source[None, :])
    earlier = earlier.astype(jnp.bfloat16)

    def selection(known, flip):
        side = core ^ flip
        step = jnp.where(side == 0, EXCHANGE[0], EXCHANGE[1])
        base = [jnp.where(side == 0, jnp.where(v < 2, v, v ^ 3), v & 2) for v in at]
        spot = [base[i] ^ (bits[:, i] * step) for i in range(3)]
        wanted = index_of(spot[0], core, spot[1], spot[2])[:, None].astype(jnp.float32)
        known = known.astype(jnp.float32).T[: 2 * top].reshape(2, top, held)
        named = jnp.zeros((corners, held), jnp.float32)
        weight = named
        for k in range(top):
            same = wanted == known[0, k][None, :]
            named = jnp.where(same, jnp.float32(1.0), named)
            weight = jnp.where(same, known[1, k][None, :], weight)
        slot = jnp.dot(named.astype(jnp.bfloat16), earlier, preferred_element_type=jnp.float32)
        slot = jnp.where(named > 0.0, slot, jnp.float32(-1.0))
        chosen = slot[:, None, :] == jnp.arange(cap, dtype=jnp.float32)[None, :, None]
        weights = jnp.where(chosen, weight[:, None, :], jnp.float32(0.0))
        wide = []
        for small in (chosen.astype(jnp.float32), weights):
            small = jnp.where(mask[None], small[:, None], jnp.float32(0.0)).astype(jnp.bfloat16)
            wide.append(small.reshape(corners * corners * cap, held))
        return wide

    flat = (corners * corners * cap, width)
    boxed = (corners, corners * cap, width)
    experts_of = (expert_gate[0], expert_up[0], expert_down[0])

    def send(held, known, flip):
        chosen, weights = selection(known, flip)
        picked = jnp.dot(chosen, held, preferred_element_type=jnp.float32).astype(jnp.bfloat16)
        return exchange(picked.reshape(boxed), flip).reshape(flat), weights

    def collect(back, weights):
        total = lax.dot_general(weights, back, (((0,), (0,)), ((), ())), preferred_element_type=jnp.float32)
        return total.astype(jnp.bfloat16)

    other_rows, other_weights = send(other_held, other_known, 1)
    own_rows, own_weights = send(own_held, own_known, 0)
    other_out = follow(expert(other_rows, *experts_of, expert_ids), own_rows)
    other_back = exchange(other_out.reshape(boxed), 1).reshape(flat)
    own_out = follow(expert(own_rows, *experts_of, other_out), other_back)
    own_back = exchange(own_out.reshape(boxed), 0).reshape(flat)
    other_total = to_other_core(follow(collect(other_back, other_weights), own_out))
    own_total = collect(own_back, own_weights)
    total = add(own_total, other_total)
    return reduce_cube([total[i * tok : (i + 1) * tok] for i in range(corners)])


def solution(mesh):
    placed = (
        P(("node", "local"), None),
        P(("node", "local"), None),
        P(("node", "local"), None),
        P(("node", "local"), None, None),
        P(("node", "local"), None, None),
        P(("node", "local"), None, None),
    )
    return jax.shard_map(
        shards, mesh=mesh, in_specs=placed, out_specs=P(("node", "local"), None), check_vma=False
    )
```

```python
import functools

import jax
import jax.numpy as jnp
from jax import lax
from jax.experimental import pallas as pl
from jax.experimental.pallas import tpu as pltpu
from jax.sharding import PartitionSpec as P

BOTH = ("node", "local")
RING = 4
CORES = 2
LANES = 128

GATHER = (1, 3)
EXCHANGE = (3, 1)

NEAR = ((0, 0, 0), (1, 0, 0), (0, 1, 0), (0, 0, 1))
FAR = ((1, 1, 0), (0, 1, 1), (1, 0, 1), (1, 1, 1))
CORNERS = tuple((i >> 2 & 1, i >> 1 & 1, i & 1) for i in range(8))


def index_of(y, c, x, z):
    return ((y * CORES + c) * RING + x) * RING + z


def places():
    return [
        (y, c, x, z) for y in range(RING) for c in range(CORES) for x in range(RING) for z in range(RING)
    ]


def moved(place, corner, step):
    y, c, x, z = place
    return index_of(y ^ corner[0] * step, c, x ^ corner[1] * step, z ^ corner[2] * step)


def to_corner(value, corner):
    return lax.ppermute(value, BOTH, [(index_of(*p), moved(p, corner, GATHER[p[1]])) for p in places()])


def to_other_core(value):
    return lax.ppermute(
        value, BOTH, [(index_of(y, c, x, z), index_of(y, 1 - c, x, z)) for y, c, x, z in places()]
    )


def first_of(v, core):
    return (v if v < 2 else v ^ 3) if core == 0 else v & 2


def exchange(value, flip):
    groups = [
        [moved((y, c, x, z), corner, EXCHANGE[c ^ flip]) for corner in CORNERS]
        for y, c, x, z in places()
        if all(first_of(v, c ^ flip) == v for v in (y, x, z))
    ]
    return lax.all_to_all(
        value, BOTH, split_axis=0, concat_axis=0, axis_index_groups=groups, tiled=True
    )


def gather_cube(block):
    y, x, z = [to_corner(block, corner) for corner in NEAR[1:]]
    far = [to_corner(x, NEAR[1]), to_corner(z, NEAR[2]), to_corner(y, NEAR[3]), to_corner(block, FAR[3])]
    return [block, y, x, z] + far


def add(a, *others):
    total = a.astype(jnp.float32)
    for b in others:
        total = total + b.astype(jnp.float32)
    return total.astype(jnp.bfloat16)


def reduce_cube(blocks):
    own, y, x, z, yx, xz, yz, yxz = blocks
    x = add(x, to_corner(yx, NEAR[1]))
    z = add(z, to_corner(xz, NEAR[2]))
    y = add(y, to_corner(yz, NEAR[3]))
    last = to_corner(yxz, FAR[3])
    return add(own, last, *[to_corner(b, corner) for b, corner in zip((y, x, z), NEAR[1:])])


def select_kernel(count, tok, top, *refs):
    wanted_ref, earlier_ref = refs[:2]
    blocks, labels, outs, chosen = refs[2 : 2 + count], refs[2 + count : 2 + 2 * count], refs[2 + 2 * count : -1], refs[-1]
    members = wanted_ref.shape[0]
    cap = chosen.shape[0] // members**2

    def whole(parts):
        parts = [part[...] for part in parts]
        return parts[0] if len(parts) == 1 else jnp.concatenate(parts, axis=0)

    @pl.when(pl.program_id(0) == 0)
    def _():
        known = whole(labels)
        if len(outs) > 1:
            outs[2][...] = known
        known = known.astype(jnp.float32).T
        held = known.shape[1]
        wanted = wanted_ref[...]
        named = jnp.zeros((members, held), jnp.float32)
        for k in range(top):
            named = jnp.where(wanted == known[k : k + 1], jnp.float32(1.0), named)
        slot = jnp.dot(named.astype(chosen.dtype), earlier_ref[...], preferred_element_type=jnp.float32)
        slot = jnp.where(named > 0.0, slot, jnp.float32(-1.0))
        rank = lax.broadcasted_iota(jnp.int32, (cap, held), 0).astype(jnp.float32)
        lane = lax.broadcasted_iota(jnp.int32, (cap, held), 1)
        for member in range(members):
            same = jnp.where(slot[member : member + 1] == rank, jnp.float32(1.0), jnp.float32(0.0))
            for source in range(0, members, 2):
                pair = [
                    jnp.where((lane >= i * tok) & (lane < (i + 1) * tok), same, jnp.float32(0.0))
                    for i in (source, source + 1)
                ]
                first = (member * members + source) * cap
                chosen[first : first + 2 * cap] = jnp.concatenate(pair, axis=0).astype(chosen.dtype)

    rows = whole(blocks)
    if len(outs) > 1:
        outs[1][...] = rows
    picked = jnp.dot(chosen[...], rows, preferred_element_type=jnp.float32)
    outs[0][...] = picked.astype(outs[0].dtype)


def select(wanted, earlier, blocks, labels, place, tok, top, width, keep):
    held = earlier.shape[0]
    members = wanted.shape[0]
    cap = 2 * tok * top // (CORES * RING**3)
    count = members * members * cap
    wide = 896
    dtype = blocks[0].dtype
    rows = jax.ShapeDtypeStruct((count, width), dtype)
    outs = [(rows, pl.BlockSpec((count, wide), lambda i: (0, i)))]
    if keep:
        outs.append((jax.ShapeDtypeStruct((held, width), dtype), pl.BlockSpec((held, wide), lambda i: (0, i))))
        outs.append((jax.ShapeDtypeStruct((held, LANES), dtype), pl.BlockSpec((held, LANES), lambda i: (0, 0))))
    return pl.pallas_call(
        functools.partial(select_kernel, len(blocks), tok, top),
        grid=(width // wide,),
        in_specs=[
            pl.BlockSpec(wanted.shape, lambda i: (0, 0)),
            pl.BlockSpec(earlier.shape, lambda i: (0, 0)),
        ]
        + [pl.BlockSpec((block.shape[0], wide), lambda i: (0, i)) for block in blocks]
        + [pl.BlockSpec((label.shape[0], LANES), lambda i: (0, place)) for label in labels],
        out_specs=[spec for _, spec in outs],
        out_shape=[shape for shape, _ in outs],
        scratch_shapes=[pltpu.VMEM((count, held), dtype)],
        compiler_params=pltpu.CompilerParams(vmem_limit_bytes=40 * 2**20),
        cost_estimate=pl.CostEstimate(
            flops=2 * count * held * width, bytes_accessed=6 * count * width, transcendentals=0
        ),
        name="select",
    )(wanted, earlier, *blocks, *labels)


def follow_kernel(value_ref, after_ref, out_ref):
    del value_ref, after_ref, out_ref


def follow(value, after):
    return pl.pallas_call(
        follow_kernel,
        in_specs=[pl.BlockSpec(memory_space=pl.ANY)] * 2,
        out_specs=pl.BlockSpec(memory_space=pl.ANY),
        out_shape=jax.ShapeDtypeStruct(value.shape, value.dtype),
        input_output_aliases={0: 0},
        name="follow",
    )(value, after)


def expert_kernel(inner, tile, rows_ref, gate_ref, up_ref, down_ref, *refs):
    out_ref, hidden = refs[-2:]
    step = pl.program_id(0)

    @pl.when(step < inner)
    def _():
        gate = jnp.dot(rows_ref[...], gate_ref[...], preferred_element_type=jnp.float32)
        up = jnp.dot(rows_ref[...], up_ref[...], preferred_element_type=jnp.float32)
        columns = pl.ds(pl.multiple_of(step * tile, tile), tile)
        hidden[:, columns] = (gate / (1.0 + jnp.exp(-gate)) * up).astype(hidden.dtype)

    @pl.when(step >= inner)
    def _():
        out = jnp.dot(hidden[...], down_ref[...], preferred_element_type=jnp.float32)
        out_ref[...] = out.astype(out_ref.dtype)


def expert(rows, gate, up, down, after):
    count, width = rows.shape
    hidden = gate.shape[1]
    tile = 256
    wide = 512
    inner, outer = hidden // tile, width // wide

    def of_inner(i):
        return 0, jnp.minimum(i, inner - 1)

    def of_outer(i):
        return 0, jnp.maximum(i - inner, 0)

    return pl.pallas_call(
        functools.partial(expert_kernel, inner, tile),
        grid=(inner + outer,),
        in_specs=[
            pl.BlockSpec((count, width), lambda i: (0, 0)),
            pl.BlockSpec((width, tile), of_inner),
            pl.BlockSpec((width, tile), of_inner),
            pl.BlockSpec((hidden, wide), of_outer),
        ]
        + [pl.BlockSpec(memory_space=pl.ANY)] * len(after),
        out_specs=pl.BlockSpec((count, wide), of_outer),
        out_shape=jax.ShapeDtypeStruct((count, width), rows.dtype),
        scratch_shapes=[pltpu.VMEM((count, hidden), rows.dtype)],
        compiler_params=pltpu.CompilerParams(vmem_limit_bytes=48 * 2**20),
        cost_estimate=pl.CostEstimate(
            flops=6 * count * width * hidden,
            bytes_accessed=2 * (3 * width * hidden + 2 * count * width),
            transcendentals=count * hidden,
        ),
        name="expert",
    )(rows, gate, up, down, *after)


def shards(tokens, expert_ids, gate_values, expert_gate, expert_up, expert_down):
    node = lax.axis_index("node")
    local = lax.axis_index("local")
    at = (node // CORES, local // RING, local % RING)
    core = node % CORES
    experts = lax.axis_size("node") * lax.axis_size("local")
    tok, width = tokens.shape
    top = expert_ids.shape[1]
    cap = 2 * tok * top // experts
    corners = len(CORNERS)
    held = corners * tok

    about = jnp.concatenate([expert_ids.astype(jnp.bfloat16), gate_values], axis=1)
    about = jnp.pad(about, ((0, 0), (0, LANES - 2 * top)))
    blocks = gather_cube(jnp.concatenate([tokens, about], axis=1))

    bits = jnp.array(CORNERS, dtype=jnp.int32)
    source = jnp.repeat(jnp.arange(corners, dtype=jnp.int32), tok)
    mask = jnp.arange(corners, dtype=jnp.int32)[:, None, None] == source[None, None, :]
    order = jnp.arange(held, dtype=jnp.int32)
    earlier = (order[:, None] < order[None, :]) & (source[:, None] == source[None, :])
    earlier = earlier.astype(jnp.bfloat16)

    def experts_for(flip):
        side = core ^ flip
        step = jnp.where(side == 0, EXCHANGE[0], EXCHANGE[1])
        base = [jnp.where(side == 0, jnp.where(v < 2, v, v ^ 3), v & 2) for v in at]
        spot = [base[i] ^ (bits[:, i] * step) for i in range(3)]
        return index_of(spot[0], core, spot[1], spot[2])[:, None].astype(jnp.float32)

    def weights_of(wanted, known):
        known = known.astype(jnp.float32).T[: 2 * top].reshape(2, top, held)
        named = jnp.zeros((corners, held), jnp.float32)
        weight = named
        for k in range(top):
            same = wanted == known[0, k][None, :]
            named = jnp.where(same, jnp.float32(1.0), named)
            weight = jnp.where(same, known[1, k][None, :], weight)
        slot = jnp.dot(named.astype(jnp.bfloat16), earlier, preferred_element_type=jnp.float32)
        slot = jnp.where(named > 0.0, slot, jnp.float32(-1.0))
        chosen = slot[:, None, :] == jnp.arange(cap, dtype=jnp.float32)[None, :, None]
        weights = jnp.where(chosen, weight[:, None, :], jnp.float32(0.0))
        weights = jnp.where(mask[None], weights[:, None], jnp.float32(0.0)).astype(jnp.bfloat16)
        return weights.reshape(corners * corners * cap, held)

    flat = (corners * corners * cap, width)
    boxed = (corners, corners * cap, width)
    experts_of = (expert_gate[0], expert_up[0], expert_down[0])

    def collect(back, weights):
        total = lax.dot_general(weights, back, (((0,), (0,)), ((), ())), preferred_element_type=jnp.float32)
        return total.astype(jnp.bfloat16)

    own_experts, other_experts = experts_for(0), experts_for(1)
    own_picked, own_held, own_known = select(
        own_experts, earlier, blocks, blocks, width // LANES, tok, top, width, True
    )
    own_rows = exchange(own_picked.reshape(boxed), 0).reshape(flat)
    other_held, other_known = to_other_core(own_held), to_other_core(own_known)
    other_picked = select(other_experts, earlier, [other_held], [other_known], 0, tok, top, width, False)[0]
    other_rows = exchange(other_picked.reshape(boxed), 1).reshape(flat)
    own_weights = weights_of(own_experts, own_known)
    other_weights = weights_of(other_experts, other_known)
    own_out = follow(expert(own_rows, *experts_of, [own_weights, other_weights]), other_rows)
    own_back = exchange(own_out.reshape(boxed), 0).reshape(flat)
    other_out = follow(expert(other_rows, *experts_of, [own_out]), own_back)
    other_back = exchange(other_out.reshape(boxed), 1).reshape(flat)
    own_total = collect(own_back, own_weights)
    half = held // 2
    far = to_other_core(collect(other_back, other_weights[:, half:]))
    near = to_other_core(collect(other_back, other_weights[:, :half]))
    total = [add(own_total[i * tok : (i + 1) * tok], near[i * tok : (i + 1) * tok]) for i in range(corners // 2)]
    total += [add(own_total[half + i * tok :][:tok], far[i * tok : (i + 1) * tok]) for i in range(corners // 2)]
    return reduce_cube(total)


def solution(mesh):
    placed = (
        P(("node", "local"), None),
        P(("node", "local"), None),
        P(("node", "local"), None),
        P(("node", "local"), None, None),
        P(("node", "local"), None, None),
        P(("node", "local"), None, None),
    )
    return jax.shard_map(
        shards, mesh=mesh, in_specs=placed, out_specs=P(("node", "local"), None), check_vma=False
    )
```

```python
import functools

import jax
import jax.numpy as jnp
from jax import lax
from jax.experimental import pallas as pl
from jax.experimental.pallas import tpu as pltpu
from jax.sharding import PartitionSpec as P

BOTH = ("node", "local")
RING = 4
CORES = 2
LANES = 128

GATHER = (1, 3)
EXCHANGE = (3, 1)

NEAR = ((0, 0, 0), (1, 0, 0), (0, 1, 0), (0, 0, 1))
FAR = ((1, 1, 0), (0, 1, 1), (1, 0, 1), (1, 1, 1))
CORNERS = tuple((i >> 2 & 1, i >> 1 & 1, i & 1) for i in range(8))


def index_of(y, c, x, z):
    return ((y * CORES + c) * RING + x) * RING + z


def places():
    return [
        (y, c, x, z) for y in range(RING) for c in range(CORES) for x in range(RING) for z in range(RING)
    ]


def moved(place, corner, step):
    y, c, x, z = place
    return index_of(y ^ corner[0] * step, c, x ^ corner[1] * step, z ^ corner[2] * step)


def to_corner(value, corner):
    return lax.ppermute(value, BOTH, [(index_of(*p), moved(p, corner, GATHER[p[1]])) for p in places()])


def to_other_core(value):
    return lax.ppermute(
        value, BOTH, [(index_of(y, c, x, z), index_of(y, 1 - c, x, z)) for y, c, x, z in places()]
    )


def first_of(v, core):
    return (v if v < 2 else v ^ 3) if core == 0 else v & 2


def exchange(value, flip):
    groups = [
        [moved((y, c, x, z), corner, EXCHANGE[c ^ flip]) for corner in CORNERS]
        for y, c, x, z in places()
        if all(first_of(v, c ^ flip) == v for v in (y, x, z))
    ]
    return lax.all_to_all(
        value, BOTH, split_axis=0, concat_axis=0, axis_index_groups=groups, tiled=True
    )


def gather_cube(block):
    y, x, z = [to_corner(block, corner) for corner in NEAR[1:]]
    far = [to_corner(x, NEAR[1]), to_corner(z, NEAR[2]), to_corner(y, NEAR[3]), to_corner(block, FAR[3])]
    return [block, y, x, z] + far


def add(a, *others):
    total = a.astype(jnp.float32)
    for b in others:
        total = total + b.astype(jnp.float32)
    return total.astype(jnp.bfloat16)


def reduce_cube(blocks):
    own, y, x, z, yx, xz, yz, yxz = blocks
    x = add(x, to_corner(yx, NEAR[1]))
    z = add(z, to_corner(xz, NEAR[2]))
    y = add(y, to_corner(yz, NEAR[3]))
    last = to_corner(yxz, FAR[3])
    return add(own, last, *[to_corner(b, corner) for b, corner in zip((y, x, z), NEAR[1:])])


def select_kernel(count, tok, top, *refs):
    wanted_ref, earlier_ref = refs[:2]
    blocks, labels, outs, chosen = refs[2 : 2 + count], refs[2 + count : 2 + 2 * count], refs[2 + 2 * count : -1], refs[-1]
    members = wanted_ref.shape[0]
    cap = chosen.shape[0] // members**2

    def whole(parts):
        parts = [part[...] for part in parts]
        return parts[0] if len(parts) == 1 else jnp.concatenate(parts, axis=0)

    @pl.when(pl.program_id(0) == 0)
    def _():
        known = whole(labels)
        if len(outs) > 1:
            outs[2][...] = known
        known = known.astype(jnp.float32).T
        held = known.shape[1]
        wanted = wanted_ref[...]
        named = jnp.zeros((members, held), jnp.float32)
        for k in range(top):
            named = jnp.where(wanted == known[k : k + 1], jnp.float32(1.0), named)
        slot = jnp.dot(named.astype(chosen.dtype), earlier_ref[...], preferred_element_type=jnp.float32)
        slot = jnp.where(named > 0.0, slot, jnp.float32(-1.0))
        rank = lax.broadcasted_iota(jnp.int32, (cap, held), 0).astype(jnp.float32)
        lane = lax.broadcasted_iota(jnp.int32, (cap, held), 1)
        for member in range(members):
            same = jnp.where(slot[member : member + 1] == rank, jnp.float32(1.0), jnp.float32(0.0))
            for source in range(0, members, 2):
                pair = [
                    jnp.where((lane >= i * tok) & (lane < (i + 1) * tok), same, jnp.float32(0.0))
                    for i in (source, source + 1)
                ]
                first = (member * members + source) * cap
                chosen[first : first + 2 * cap] = jnp.concatenate(pair, axis=0).astype(chosen.dtype)

    rows = whole(blocks)
    if len(outs) > 1:
        outs[1][...] = rows
    picked = jnp.dot(chosen[...], rows, preferred_element_type=jnp.float32)
    outs[0][...] = picked.astype(outs[0].dtype)


def select(wanted, earlier, blocks, labels, place, tok, top, width, keep):
    held = earlier.shape[0]
    members = wanted.shape[0]
    cap = 2 * tok * top // (CORES * RING**3)
    count = members * members * cap
    wide = 1792
    dtype = blocks[0].dtype
    rows = jax.ShapeDtypeStruct((count, width), dtype)
    outs = [(rows, pl.BlockSpec((count, wide), lambda i: (0, i)))]
    if keep:
        outs.append((jax.ShapeDtypeStruct((held, width), dtype), pl.BlockSpec((held, wide), lambda i: (0, i))))
        outs.append((jax.ShapeDtypeStruct((held, LANES), dtype), pl.BlockSpec((held, LANES), lambda i: (0, 0))))
    return pl.pallas_call(
        functools.partial(select_kernel, len(blocks), tok, top),
        grid=(width // wide,),
        in_specs=[
            pl.BlockSpec(wanted.shape, lambda i: (0, 0)),
            pl.BlockSpec(earlier.shape, lambda i: (0, 0)),
        ]
        + [pl.BlockSpec((block.shape[0], wide), lambda i: (0, i)) for block in blocks]
        + [pl.BlockSpec((label.shape[0], LANES), lambda i: (0, place)) for label in labels],
        out_specs=[spec for _, spec in outs],
        out_shape=[shape for shape, _ in outs],
        scratch_shapes=[pltpu.VMEM((count, held), dtype)],
        compiler_params=pltpu.CompilerParams(vmem_limit_bytes=60 * 2**20),
        cost_estimate=pl.CostEstimate(
            flops=2 * count * held * width, bytes_accessed=6 * count * width, transcendentals=0
        ),
        name="select",
    )(wanted, earlier, *blocks, *labels)


def follow_kernel(value_ref, after_ref, out_ref):
    del value_ref, after_ref, out_ref


def follow(value, after):
    return pl.pallas_call(
        follow_kernel,
        in_specs=[pl.BlockSpec(memory_space=pl.ANY)] * 2,
        out_specs=pl.BlockSpec(memory_space=pl.ANY),
        out_shape=jax.ShapeDtypeStruct(value.shape, value.dtype),
        input_output_aliases={0: 0},
        name="follow",
    )(value, after)


def expert_kernel(inner, tile, rows_ref, gate_ref, up_ref, down_ref, *refs):
    out_ref, hidden = refs[-2:]
    step = pl.program_id(0)

    @pl.when(step < inner)
    def _():
        gate = jnp.dot(rows_ref[...], gate_ref[...], preferred_element_type=jnp.float32)
        up = jnp.dot(rows_ref[...], up_ref[...], preferred_element_type=jnp.float32)
        columns = pl.ds(pl.multiple_of(step * tile, tile), tile)
        hidden[:, columns] = (gate / (1.0 + jnp.exp(-gate)) * up).astype(hidden.dtype)

    @pl.when(step >= inner)
    def _():
        out = jnp.dot(hidden[...], down_ref[...], preferred_element_type=jnp.float32)
        out_ref[...] = out.astype(out_ref.dtype)


def expert(rows, gate, up, down, after):
    count, width = rows.shape
    hidden = gate.shape[1]
    tile = 256
    wide = 512
    inner, outer = hidden // tile, width // wide

    def of_inner(i):
        return 0, jnp.minimum(i, inner - 1)

    def of_outer(i):
        return 0, jnp.maximum(i - inner, 0)

    return pl.pallas_call(
        functools.partial(expert_kernel, inner, tile),
        grid=(inner + outer,),
        in_specs=[
            pl.BlockSpec((count, width), lambda i: (0, 0)),
            pl.BlockSpec((width, tile), of_inner),
            pl.BlockSpec((width, tile), of_inner),
            pl.BlockSpec((hidden, wide), of_outer),
        ]
        + [pl.BlockSpec(memory_space=pl.ANY)] * len(after),
        out_specs=pl.BlockSpec((count, wide), of_outer),
        out_shape=jax.ShapeDtypeStruct((count, width), rows.dtype),
        scratch_shapes=[pltpu.VMEM((count, hidden), rows.dtype)],
        compiler_params=pltpu.CompilerParams(vmem_limit_bytes=48 * 2**20),
        cost_estimate=pl.CostEstimate(
            flops=6 * count * width * hidden,
            bytes_accessed=2 * (3 * width * hidden + 2 * count * width),
            transcendentals=count * hidden,
        ),
        name="expert",
    )(rows, gate, up, down, *after)


def shards(tokens, expert_ids, gate_values, expert_gate, expert_up, expert_down):
    node = lax.axis_index("node")
    local = lax.axis_index("local")
    at = (node // CORES, local // RING, local % RING)
    core = node % CORES
    experts = lax.axis_size("node") * lax.axis_size("local")
    tok, width = tokens.shape
    top = expert_ids.shape[1]
    cap = 2 * tok * top // experts
    corners = len(CORNERS)
    held = corners * tok

    rest = jnp.zeros((tok, LANES - 2 * top), jnp.bfloat16)
    blocks = gather_cube(jnp.concatenate([tokens, expert_ids.astype(jnp.bfloat16), gate_values, rest], axis=1))

    bits = jnp.array(CORNERS, dtype=jnp.int32)
    source = jnp.repeat(jnp.arange(corners, dtype=jnp.int32), tok)
    mask = jnp.arange(corners, dtype=jnp.int32)[:, None, None] == source[None, None, :]
    order = jnp.arange(held, dtype=jnp.int32)
    earlier = (order[:, None] < order[None, :]) & (source[:, None] == source[None, :])
    earlier = earlier.astype(jnp.bfloat16)

    def experts_for(flip):
        side = core ^ flip
        step = jnp.where(side == 0, EXCHANGE[0], EXCHANGE[1])
        base = [jnp.where(side == 0, jnp.where(v < 2, v, v ^ 3), v & 2) for v in at]
        spot = [base[i] ^ (bits[:, i] * step) for i in range(3)]
        return index_of(spot[0], core, spot[1], spot[2])[:, None].astype(jnp.float32)

    def weights_of(wanted, known):
        known = known.astype(jnp.float32).T[: 2 * top].reshape(2, top, held)
        named = jnp.zeros((corners, held), jnp.float32)
        weight = named
        for k in range(top):
            same = wanted == known[0, k][None, :]
            named = jnp.where(same, jnp.float32(1.0), named)
            weight = jnp.where(same, known[1, k][None, :], weight)
        slot = jnp.dot(named.astype(jnp.bfloat16), earlier, preferred_element_type=jnp.float32)
        slot = jnp.where(named > 0.0, slot, jnp.float32(-1.0))
        chosen = slot[:, None, :] == jnp.arange(cap, dtype=jnp.float32)[None, :, None]
        weights = jnp.where(chosen, weight[:, None, :], jnp.float32(0.0))
        weights = jnp.where(mask[None], weights[:, None], jnp.float32(0.0)).astype(jnp.bfloat16)
        return weights.reshape(corners * corners * cap, held)

    flat = (corners * corners * cap, width)
    boxed = (corners, corners * cap, width)
    experts_of = (expert_gate[0], expert_up[0], expert_down[0])

    def collect(back, weights):
        total = lax.dot_general(weights, back, (((0,), (0,)), ((), ())), preferred_element_type=jnp.float32)
        return total.astype(jnp.bfloat16)

    own_experts, other_experts = experts_for(0), experts_for(1)
    own_picked, own_held, own_known = select(
        own_experts, earlier, blocks, blocks, width // LANES, tok, top, width, True
    )
    own_rows = exchange(own_picked.reshape(boxed), 0).reshape(flat)
    other_held, other_known = to_other_core(own_held), to_other_core(own_known)
    other_picked = select(other_experts, earlier, [other_held], [other_known], 0, tok, top, width, False)[0]
    other_rows = exchange(other_picked.reshape(boxed), 1).reshape(flat)
    own_weights = weights_of(own_experts, own_known)
    other_weights = weights_of(other_experts, other_known)
    own_out = follow(expert(own_rows, *experts_of, [own_weights, other_weights]), other_rows)
    own_back = exchange(own_out.reshape(boxed), 0).reshape(flat)
    other_out = follow(expert(other_rows, *experts_of, [own_out]), own_back)
    other_back = exchange(other_out.reshape(boxed), 1).reshape(flat)
    own_total = collect(own_back, own_weights)
    half = held // 2
    far = to_other_core(collect(other_back, other_weights[:, half:]))
    near = to_other_core(collect(other_back, other_weights[:, :half]))
    total = [add(own_total[i * tok : (i + 1) * tok], near[i * tok : (i + 1) * tok]) for i in range(corners // 2)]
    total += [add(own_total[half + i * tok :][:tok], far[i * tok : (i + 1) * tok]) for i in range(corners // 2)]
    return reduce_cube(total)


def solution(mesh):
    placed = (
        P(("node", "local"), None),
        P(("node", "local"), None),
        P(("node", "local"), None),
        P(("node", "local"), None, None),
        P(("node", "local"), None, None),
        P(("node", "local"), None, None),
    )
    return jax.shard_map(
        shards, mesh=mesh, in_specs=placed, out_specs=P(("node", "local"), None), check_vma=False
    )
```

```python
import functools

import jax
import jax.numpy as jnp
from jax import lax
from jax.experimental import pallas as pl
from jax.experimental.pallas import tpu as pltpu
from jax.sharding import PartitionSpec as P

BOTH = ("node", "local")
RING = 4
CORES = 2
LANES = 128

GATHER = (1, 3)
EXCHANGE = (3, 1)

NEAR = ((0, 0, 0), (1, 0, 0), (0, 1, 0), (0, 0, 1))
FAR = ((1, 1, 0), (0, 1, 1), (1, 0, 1), (1, 1, 1))
CORNERS = tuple((i >> 2 & 1, i >> 1 & 1, i & 1) for i in range(8))


def index_of(y, c, x, z):
    return ((y * CORES + c) * RING + x) * RING + z


def places():
    return [
        (y, c, x, z) for y in range(RING) for c in range(CORES) for x in range(RING) for z in range(RING)
    ]


def moved(place, corner, step):
    y, c, x, z = place
    return index_of(y ^ corner[0] * step, c, x ^ corner[1] * step, z ^ corner[2] * step)


def to_corner(value, corner):
    return lax.ppermute(value, BOTH, [(index_of(*p), moved(p, corner, GATHER[p[1]])) for p in places()])


def to_other_core(value):
    return lax.ppermute(
        value, BOTH, [(index_of(y, c, x, z), index_of(y, 1 - c, x, z)) for y, c, x, z in places()]
    )


def first_of(v, core):
    return (v if v < 2 else v ^ 3) if core == 0 else v & 2


def exchange(value, flip):
    groups = [
        [moved((y, c, x, z), corner, EXCHANGE[c ^ flip]) for corner in CORNERS]
        for y, c, x, z in places()
        if all(first_of(v, c ^ flip) == v for v in (y, x, z))
    ]
    return lax.all_to_all(
        value, BOTH, split_axis=0, concat_axis=0, axis_index_groups=groups, tiled=True
    )


def gather_cube(block):
    y, x, z = [to_corner(block, corner) for corner in NEAR[1:]]
    far = [to_corner(x, NEAR[1]), to_corner(z, NEAR[2]), to_corner(y, NEAR[3]), to_corner(block, FAR[3])]
    return [block, y, x, z] + far


def add(a, *others):
    total = a.astype(jnp.float32)
    for b in others:
        total = total + b.astype(jnp.float32)
    return total.astype(jnp.bfloat16)


def reduce_cube(blocks):
    own, y, x, z, yx, xz, yz, yxz = blocks
    x = add(x, to_corner(yx, NEAR[1]))
    z = add(z, to_corner(xz, NEAR[2]))
    y = add(y, to_corner(yz, NEAR[3]))
    last = to_corner(yxz, FAR[3])
    return add(own, last, *[to_corner(b, corner) for b, corner in zip((y, x, z), NEAR[1:])])


def select_kernel(count, tok, top, *refs):
    wanted_ref, earlier_ref = refs[:2]
    blocks, labels, outs, chosen = refs[2 : 2 + count], refs[2 + count : 2 + 2 * count], refs[2 + 2 * count : -1], refs[-1]
    members = wanted_ref.shape[0]
    cap = chosen.shape[0] // members**2

    def whole(parts):
        parts = [part[...] for part in parts]
        return parts[0] if len(parts) == 1 else jnp.concatenate(parts, axis=0)

    @pl.when(pl.program_id(0) == 0)
    def _():
        known = whole(labels)
        if len(outs) > 1:
            outs[2][...] = known
        known = known.astype(jnp.float32).T
        held = known.shape[1]
        wanted = wanted_ref[...]
        named = jnp.zeros((members, held), jnp.float32)
        for k in range(top):
            named = jnp.where(wanted == known[k : k + 1], jnp.float32(1.0), named)
        slot = jnp.dot(named.astype(chosen.dtype), earlier_ref[...], preferred_element_type=jnp.float32)
        slot = jnp.where(named > 0.0, slot, jnp.float32(-1.0))
        rank = lax.broadcasted_iota(jnp.int32, (cap, held), 0).astype(jnp.float32)
        lane = lax.broadcasted_iota(jnp.int32, (cap, held), 1)
        for member in range(members):
            same = jnp.where(slot[member : member + 1] == rank, jnp.float32(1.0), jnp.float32(0.0))
            for source in range(0, members, 2):
                pair = [
                    jnp.where((lane >= i * tok) & (lane < (i + 1) * tok), same, jnp.float32(0.0))
                    for i in (source, source + 1)
                ]
                first = (member * members + source) * cap
                chosen[first : first + 2 * cap] = jnp.concatenate(pair, axis=0).astype(chosen.dtype)

    rows = whole(blocks)
    if len(outs) > 1:
        outs[1][...] = rows
    picked = jnp.dot(chosen[...], rows, preferred_element_type=jnp.float32)
    outs[0][...] = picked.astype(outs[0].dtype)


def select(wanted, earlier, blocks, labels, place, tok, top, width, keep):
    held = earlier.shape[0]
    members = wanted.shape[0]
    cap = 2 * tok * top // (CORES * RING**3)
    count = members * members * cap
    wide = 1792
    dtype = blocks[0].dtype
    rows = jax.ShapeDtypeStruct((count, width), dtype)
    outs = [(rows, pl.BlockSpec((count, wide), lambda i: (0, i)))]
    if keep:
        outs.append((jax.ShapeDtypeStruct((held, width), dtype), pl.BlockSpec((held, wide), lambda i: (0, i))))
        outs.append((jax.ShapeDtypeStruct((held, LANES), dtype), pl.BlockSpec((held, LANES), lambda i: (0, 0))))
    return pl.pallas_call(
        functools.partial(select_kernel, len(blocks), tok, top),
        grid=(width // wide,),
        in_specs=[
            pl.BlockSpec(wanted.shape, lambda i: (0, 0)),
            pl.BlockSpec(earlier.shape, lambda i: (0, 0)),
        ]
        + [pl.BlockSpec((block.shape[0], wide), lambda i: (0, i)) for block in blocks]
        + [pl.BlockSpec((label.shape[0], LANES), lambda i: (0, place)) for label in labels],
        out_specs=[spec for _, spec in outs],
        out_shape=[shape for shape, _ in outs],
        scratch_shapes=[pltpu.VMEM((count, held), dtype)],
        compiler_params=pltpu.CompilerParams(vmem_limit_bytes=60 * 2**20),
        cost_estimate=pl.CostEstimate(
            flops=2 * count * held * width, bytes_accessed=6 * count * width, transcendentals=0
        ),
        name="select",
    )(wanted, earlier, *blocks, *labels)


def follow_kernel(value_ref, after_ref, out_ref):
    del value_ref, after_ref, out_ref


def follow(value, after):
    return pl.pallas_call(
        follow_kernel,
        in_specs=[pl.BlockSpec(memory_space=pl.ANY)] * 2,
        out_specs=pl.BlockSpec(memory_space=pl.ANY),
        out_shape=jax.ShapeDtypeStruct(value.shape, value.dtype),
        input_output_aliases={0: 0},
        name="follow",
    )(value, after)


def expert_kernel(inner, tile, rows_ref, gate_ref, up_ref, down_ref, *refs):
    out_ref, hidden = refs[-2:]
    step = pl.program_id(0)

    @pl.when(step < inner)
    def _():
        gate = jnp.dot(rows_ref[...], gate_ref[...], preferred_element_type=jnp.float32)
        up = jnp.dot(rows_ref[...], up_ref[...], preferred_element_type=jnp.float32)
        columns = pl.ds(pl.multiple_of(step * tile, tile), tile)
        hidden[:, columns] = (gate / (1.0 + jnp.exp(-gate)) * up).astype(hidden.dtype)

    @pl.when(step >= inner)
    def _():
        out = jnp.dot(hidden[...], down_ref[...], preferred_element_type=jnp.float32)
        out_ref[...] = out.astype(out_ref.dtype)


def expert(rows, gate, up, down, after):
    count, width = rows.shape
    hidden = gate.shape[1]
    tile = 256
    wide = 512
    inner, outer = hidden // tile, width // wide

    def of_inner(i):
        return 0, jnp.minimum(i, inner - 1)

    def of_outer(i):
        return 0, jnp.maximum(i - inner, 0)

    return pl.pallas_call(
        functools.partial(expert_kernel, inner, tile),
        grid=(inner + outer,),
        in_specs=[
            pl.BlockSpec((count, width), lambda i: (0, 0)),
            pl.BlockSpec((width, tile), of_inner),
            pl.BlockSpec((width, tile), of_inner),
            pl.BlockSpec((hidden, wide), of_outer),
        ]
        + [pl.BlockSpec(memory_space=pl.ANY)] * len(after),
        out_specs=pl.BlockSpec((count, wide), of_outer),
        out_shape=jax.ShapeDtypeStruct((count, width), rows.dtype),
        scratch_shapes=[pltpu.VMEM((count, hidden), rows.dtype)],
        compiler_params=pltpu.CompilerParams(vmem_limit_bytes=48 * 2**20),
        cost_estimate=pl.CostEstimate(
            flops=6 * count * width * hidden,
            bytes_accessed=2 * (3 * width * hidden + 2 * count * width),
            transcendentals=count * hidden,
        ),
        name="expert",
    )(rows, gate, up, down, *after)


def shards(tokens, expert_ids, gate_values, expert_gate, expert_up, expert_down):
    node = lax.axis_index("node")
    local = lax.axis_index("local")
    at = (node // CORES, local // RING, local % RING)
    core = node % CORES
    experts = lax.axis_size("node") * lax.axis_size("local")
    tok, width = tokens.shape
    top = expert_ids.shape[1]
    cap = 2 * tok * top // experts
    corners = len(CORNERS)
    held = corners * tok

    rest = jnp.zeros((tok, LANES - 2 * top), jnp.bfloat16)
    blocks = gather_cube(jnp.concatenate([tokens, expert_ids.astype(jnp.bfloat16), gate_values, rest], axis=1))

    bits = jnp.array(CORNERS, dtype=jnp.int32)
    source = jnp.repeat(jnp.arange(corners, dtype=jnp.int32), tok)
    mask = jnp.arange(corners, dtype=jnp.int32)[:, None, None] == source[None, None, :]
    order = jnp.arange(held, dtype=jnp.int32)
    earlier = (order[:, None] < order[None, :]) & (source[:, None] == source[None, :])
    earlier = earlier.astype(jnp.bfloat16)

    def experts_for(flip):
        side = core ^ flip
        step = jnp.where(side == 0, EXCHANGE[0], EXCHANGE[1])
        base = [jnp.where(side == 0, jnp.where(v < 2, v, v ^ 3), v & 2) for v in at]
        spot = [base[i] ^ (bits[:, i] * step) for i in range(3)]
        return index_of(spot[0], core, spot[1], spot[2])[:, None].astype(jnp.float32)

    def weights_of(wanted, known):
        known = known.astype(jnp.float32).T[: 2 * top].reshape(2, top, held)
        named = jnp.zeros((corners, held), jnp.float32)
        weight = named
        for k in range(top):
            same = wanted == known[0, k][None, :]
            named = jnp.where(same, jnp.float32(1.0), named)
            weight = jnp.where(same, known[1, k][None, :], weight)
        slot = jnp.dot(named.astype(jnp.bfloat16), earlier, preferred_element_type=jnp.float32)
        slot = jnp.where(named > 0.0, slot, jnp.float32(-1.0))
        chosen = slot[:, None, :] == jnp.arange(cap, dtype=jnp.float32)[None, :, None]
        weights = jnp.where(chosen, weight[:, None, :], jnp.float32(0.0))
        weights = jnp.where(mask[None], weights[:, None], jnp.float32(0.0)).astype(jnp.bfloat16)
        return weights.reshape(corners * corners * cap, held)

    flat = (corners * corners * cap, width)
    boxed = (corners, corners * cap, width)
    experts_of = (expert_gate[0], expert_up[0], expert_down[0])

    def collect(back, weights):
        total = lax.dot_general(weights, back, (((0,), (0,)), ((), ())), preferred_element_type=jnp.float32)
        return total.astype(jnp.bfloat16)

    own_experts, other_experts = experts_for(0), experts_for(1)
    own_picked, own_held, own_known = select(
        own_experts, earlier, blocks, blocks, width // LANES, tok, top, width, True
    )
    own_rows = exchange(own_picked.reshape(boxed), 0).reshape(flat)
    other_held, other_known = to_other_core(own_held), to_other_core(own_known)
    other_picked = select(other_experts, earlier, [other_held], [other_known], 0, tok, top, width, False)[0]
    other_rows = exchange(other_picked.reshape(boxed), 1).reshape(flat)
    own_weights = weights_of(own_experts, own_known)
    beside = (own_experts.astype(jnp.int32) ^ (RING * RING)).astype(jnp.float32)
    other_weights = weights_of(beside, own_known)
    own_out = follow(expert(own_rows, *experts_of, [own_weights, other_weights]), other_rows)
    own_back = exchange(own_out.reshape(boxed), 0).reshape(flat)
    other_out = follow(expert(other_rows, *experts_of, [own_out]), own_back)
    own_total = collect(own_back, own_weights)
    other_out = follow(to_other_core(other_out), own_total)
    other_back = exchange(other_out.reshape(boxed), 0).reshape(flat)
    total = add(own_total, collect(other_back, other_weights))
    return reduce_cube([total[i * tok : (i + 1) * tok] for i in range(corners)])


def solution(mesh):
    placed = (
        P(("node", "local"), None),
        P(("node", "local"), None),
        P(("node", "local"), None),
        P(("node", "local"), None, None),
        P(("node", "local"), None, None),
        P(("node", "local"), None, None),
    )
    return jax.shard_map(
        shards, mesh=mesh, in_specs=placed, out_specs=P(("node", "local"), None), check_vma=False
    )
```
